32 devices in a mesh: rep: 2 (over core), lists: 16 (over z, y, x).
Axes of the slice: x: 2, y: 2, z: 4, core: 2. Of those that a mesh axis runs over, the one named last changes fastest.
Arguments:
- queries: bfloat16 [4096, 768], P(('rep', 'lists')), may hold values from -6 to 6
- rates: bfloat16 [4096], P(('rep', 'lists')), may hold values from 1.9967556e-06 to 4.9829483e-05
- probes: int32 [4096, 8], P(('rep', 'lists')), may hold values from 0 to 31, all different within a row; in each aligned block of 128 rows (0 to 127, 128 to 255, ...) at most 64 rows name the same one
- list_place: int32 [32], replicated, may hold values from 0 to 31, each once
- items: bfloat16 [65536, 768], P('lists'), may hold values from -0.21875 to 0.21875
- ages: int32 [65536], P('lists'), may hold values from 0 to 86399
- fresh_items: bfloat16 [32768, 768], P(('rep', 'lists')), may hold values from -0.21875 to 0.21875
- fresh_ages: int32 [32768], P(('rep', 'lists')), may hold values from 0 to 7199
- owner: int32 [1], replicated, may hold values from 0 to 31
Outputs:
- block_max: float32 [4096, 128], P(('rep', 'lists'))
- fresh_max: float32 [4096, 8], P(('rep', 'lists'))
The draws below stay inside these ranges and needn't reach their ends.
Inputs may be any that keep to these rules, and one draw needn't show every extreme that they name: `probes`: within the rows of one device (aligned blocks of 128 queries) no list is probed by more than 64 queries; the 8 lists of a query differ. `list_place`: each slot once.
All inputs are finite; a program needn't handle non-finite values.
Results may differ from the reference program's by a relative error of at most 0.0003.
Values may be sent and summed in bfloat16 or wider, within the bound.
A program may use at most 128 MiB of HBM per device.

```python
import math
import jax
import jax.numpy as jnp
import numpy as np
from jax import lax

D = 768
PROBES = 8
ITEMS_BLOCK = 128
LIST_ROWS = 2048
Q_DEV = 128
FRESH = 1024
LISTS = 32
MOST = 64
BLOCKS = 16
QUERIES = 4096
BANK = 65536
FRESH_ALL = 32768
N_REP = 2
N_LISTS = 16
DEVICES = 32


def plant(drawn, own_key, smallest, largest):
    longest = drawn.shape.index(max(drawn.shape))
    spots = []
    for shift in (0, 1):
        where = [jax.random.randint(jax.random.fold_in(own_key, axis), (), 0, length) for axis, length in enumerate(drawn.shape)]
        where[longest] = (where[longest] + shift) % drawn.shape[longest]
        spots.append(tuple(where))
    return drawn.at[spots[0]].set(smallest).at[spots[1]].set(largest)


def levels(rng, dims, cuts, smallest, largest):
    loudness, own = 1.0, jax.random.fold_in(rng, 6)
    for position, parts in cuts:
        heights = jnp.exp(jax.random.uniform(jax.random.fold_in(own, position), (parts,), jnp.float32, smallest / len(cuts), largest / len(cuts)))
        loudness = loudness * jnp.repeat(heights, dims[position] // parts).reshape([-1 if axis == position else 1 for axis in range(len(dims))])
    return loudness


def routed_block(own_key, own, number, rows, number_of, top, most, skew):
    order = jax.random.permutation(own_key, number_of)
    crowded, common = load_shares(number_of, rows * top, most, skew, True), load_shares(number_of, rows * top, most, skew, False)
    places = jnp.arange(number_of)

    def named(tallies, offset_by):
        used = int((tallies > 0).sum())
        fixed = max(1, used // 4)
        moved = fixed + (places - fixed + offset_by * (used - fixed)) % max(1, number_of - fixed)
        return jnp.zeros((number_of,), jnp.int32).at[order[jnp.where(places < fixed, places, moved)]].set(jnp.asarray(tallies, jnp.int32))

    tallies = jnp.where(number % 4 == 0, named(crowded, number // 4), named(common, number - number // 4 - 1))
    mixed = jax.random.permutation(jax.random.fold_in(own, 3), number_of)
    source_of, sink = mixed[0:number_of // 2 * 2:2], mixed[1:number_of // 2 * 2:2]
    slack = jnp.minimum(tallies[source_of] - 1, most - tallies[sink]) // 2
    slack = jnp.where((source_of == order[0]) | (sink == order[0]) | (tallies[sink] == 0), 0, jnp.maximum(slack, 0))
    moved = jax.random.randint(jax.random.fold_in(own, 4), (number_of // 2,), 0, 1 << 20) % (slack + 1)
    tallies = tallies.at[source_of].add(-moved).at[sink].add(moved)
    items = jnp.searchsorted(jnp.cumsum(tallies), jnp.arange(rows * top), side="right").astype(jnp.int32)
    table = items.reshape(top, rows).T
    table = table[jax.random.permutation(jax.random.fold_in(own, 1), rows)]
    offset_by = jax.random.randint(jax.random.fold_in(own, 2), (rows, 1), 0, top)
    return jnp.take_along_axis(table, (jnp.arange(top)[None, :] + offset_by) % top, axis=1)


def load_shares(amount, total, most, lean, full):
    weights = [(1 << 20) // math.isqrt(rank ** lean) + 1 for rank in range(1, amount + 1)]
    largest = most if full else min(most, max(-(-total // amount), total * weights[0] // sum(weights)))
    least = 1 if total - largest >= amount - 1 else 0
    holding, surplus = [largest] + [least] * (amount - 1), total - largest - least * (amount - 1)
    while surplus > 0:
        candidates = [i for i in range(1, amount) if holding[i] < largest] or [i for i in range(1, amount) if holding[i] < most]
        mass, remaining = sum([weights[i] for i in candidates]), surplus
        for i in candidates:
            extra = min(most - holding[i], max(1, remaining * weights[i] // mass), surplus)
            holding[i] = holding[i] + extra
            surplus = surplus - extra
    return np.array(holding)


def normal_values(stream_key, extent, width, bound, cuts=(), kind=jnp.bfloat16):
    result = jax.random.normal(stream_key, extent, jnp.float32) * width
    if len(cuts) > 0:
        result = levels(stream_key, extent, cuts, -0.22, 0.18) * result
    return jnp.clip(result, min=-bound, max=bound).astype(kind)


def setup_inputs(seed: int = 0) -> dict:
    splits = jax.random.split(jax.random.key(seed), 10)
    queries = normal_values(splits[0], (QUERIES, D), 1.0, 6.0, ((0, 32),))
    rates = jnp.clip(jnp.exp(math.log(4.982948303222656e-05) - 3.2170832 * jax.random.uniform(splits[1], (QUERIES,), jnp.float32) ** levels(splits[1], (QUERIES,), ((0, 32),), -0.2, 0.2)), 1.996755599975586e-06, 4.982948303222656e-05).astype(jnp.bfloat16)
    probes_keys = jax.random.split(jax.random.fold_in(splits[2], 1), QUERIES // Q_DEV)
    probes_turns = jax.random.permutation(jax.random.fold_in(splits[2], 3), QUERIES // Q_DEV)
    probes = jax.vmap(lambda own, number: routed_block(jax.random.fold_in(splits[2], 2), own, number, Q_DEV, LISTS, PROBES, MOST, 2))(probes_keys, probes_turns).reshape((QUERIES, PROBES))
    list_place = jax.random.permutation(splits[3], LISTS).astype(jnp.int32)
    items = normal_values(splits[4], (BANK, D), D ** -0.5, 0.21875, ((0, 16),))
    ages = plant(jax.random.randint(splits[5], (BANK,), 0, 86400), jax.random.fold_in(splits[5], 1), 0, 86399).astype(jnp.int32)
    fresh_items = normal_values(splits[6], (FRESH_ALL, D), D ** -0.5, 0.21875, ((0, 32),))
    fresh_ages = plant(jax.random.randint(splits[7], (FRESH_ALL,), 0, 7200), jax.random.fold_in(splits[7], 1), 0, 7199).astype(jnp.int32)
    owner = jax.random.randint(splits[8], (1,), 0, DEVICES).astype(jnp.int32)
    return {"queries": queries, "rates": rates, "probes": probes, "list_place": list_place, "items": items, "ages": ages, "fresh_items": fresh_items, "fresh_ages": fresh_ages, "owner": owner}


def block_best(rows, row_rates, item_rows, item_ages):
    dots = jnp.dot(rows.astype(jnp.float32), item_rows.astype(jnp.float32).T, preferred_element_type=jnp.float32)
    decay = jnp.exp(-row_rates.astype(jnp.float32)[:, None] * item_ages.astype(jnp.float32)[None, :])
    scored = dots * decay
    return jnp.max(scored.reshape(rows.shape[0], -1, ITEMS_BLOCK), axis=2)


def reference(queries, rates, probes, list_place, items, ages, fresh_items, fresh_ages, owner):
    blocks_total = N_REP * N_LISTS
    per_block = Q_DEV * PROBES
    flat = probes.reshape(blocks_total, per_block)
    lists_iota = jnp.arange(LISTS, dtype=jnp.int32)

    def ranks(block):
        where_to = jnp.sum(jnp.where(block[:, None] == lists_iota[None, :], list_place[None, :], 0), axis=1).astype(jnp.int32)
        onehot = (where_to[:, None] == lists_iota[None, :]).astype(jnp.int32)
        earlier = jnp.cumsum(onehot, axis=0) - onehot
        return where_to, jnp.sum(earlier * onehot, axis=1).astype(jnp.int32)

    where_to, rank = lax.map(ranks, flat)
    block_ids = jnp.arange(blocks_total, dtype=jnp.int32)[:, None]
    index = ((where_to * blocks_total + block_ids) * MOST + rank).reshape(-1)
    row_of = jnp.full((LISTS * blocks_total * MOST,), blocks_total * per_block, jnp.int32)
    row_of = row_of.at[index].set(jnp.arange(blocks_total * per_block, dtype=jnp.int32))
    padded_q = jnp.concatenate([queries, jnp.zeros((1, D), queries.dtype)], axis=0)
    padded_r = jnp.concatenate([rates, jnp.zeros((1,), rates.dtype)], axis=0)
    chosen = (row_of // PROBES).reshape(LISTS, blocks_total * MOST)
    item_rows = items.reshape(LISTS, LIST_ROWS, D)
    item_ages = ages.reshape(LISTS, LIST_ROWS)

    def one_list(packed):
        picked, rows_here, ages_here = packed
        return block_best(padded_q[picked], padded_r[picked], rows_here, ages_here)

    best = lax.map(one_list, (chosen, item_rows, item_ages))
    block_max = best.reshape(-1, BLOCKS)[index].reshape(QUERIES, PROBES * BLOCKS)
    start = (owner[0] * FRESH).astype(jnp.int32)
    fresh = lax.dynamic_slice_in_dim(fresh_items, start, FRESH, 0)
    fresh_age = lax.dynamic_slice_in_dim(fresh_ages, start, FRESH, 0)
    fresh_max = block_best(queries, rates, fresh, fresh_age)
    return block_max, fresh_max
```

```python
import functools
import math

import jax
import jax.numpy as jnp
from jax import lax
from jax.experimental import pallas as pl
from jax.experimental.pallas import tpu as pltpu
from jax.sharding import PartitionSpec as P

ITEMS_BLOCK = 128
CHUNK = 1024
LOG2E = math.log2(math.e)
MESH = pl.DeviceIdType.MESH


def grid_of(n):
    if n == 16:
        return 4, 2, 2
    if n == 128:
        return 4, 4, 8
    return n, 1, 1


def kernel(
    n, dims, lists_n, per_dev,
    owner_ref, place_ref, rates_ref, probes_ref, ages_ref, fages_ref, q_ref, items_ref, fresh_ref,
    out_ref, fout_ref,
    gath, qp, item_v, fresh_v, fage_v, age_v, rate_s, rate_v, slot_v, res, ans,
    s_line, s_b, s_c, s_hb, s_hc, s_res, s_rate, r_q, r_res, r_rate, f_sem, l_sem,
):
    A, B, C = dims
    me = lax.axis_index("lists")
    rep = lax.axis_index("rep")
    a, b, c = me // (B * C), (me // C) % B, me % C
    rows = q_ref.shape[0]
    half = rows // 2
    list_rows = item_v.shape[0] // per_dev
    blocks = list_rows // ITEMS_BLOCK
    main_rows = per_dev * blocks

    def at(j, db, dc):
        return ((a + j) % A) * (B * C) + ((b + db) % B) * C + (c + dc) % C

    def remote(src, dst, ss, rs, to):
        return pltpu.make_async_remote_copy(
            src_ref=src, dst_ref=dst, send_sem=ss, recv_sem=rs,
            device_id=(rep, to), device_id_type=MESH,
        )

    barrier = pltpu.get_barrier_semaphore()

    @pl.loop(1, n)
    def _(i):
        pl.semaphore_signal(barrier, inc=1, device_id=(rep, (me + i) % n), device_id_type=MESH)

    pl.semaphore_signal(barrier, inc=1, device_id=(1 - rep, me), device_id_type=MESH)

    own_q = pltpu.make_async_copy(q_ref, gath.at[me], l_sem.at[0])
    own_items = pltpu.make_async_copy(items_ref, item_v, l_sem.at[1])
    own_fresh = pltpu.make_async_copy(fresh_ref, fresh_v.at[0], l_sem.at[2])
    own_q.start()
    own_items.start()
    own_fresh.start()
    rate_s[...] = jnp.broadcast_to(rates_ref[...].astype(jnp.float32) * (-LOG2E), rate_s.shape)
    pl.semaphore_wait(barrier, n)

    def line_send(j):
        return remote(q_ref, gath.at[me], s_line.at[j], r_q.at[me, 0], at(j, 0, 0))

    def column(j, first):
        s = at(j, 0, 0)
        return q_ref if first else gath.at[s]

    def b_send(j, db, first=False):
        s = at(j, 0, 0)
        return remote(column(j, first), gath.at[s], s_b.at[j, db], r_q.at[s, 0], at(0, db, 0))

    def c_send(j, dc, first=False):
        s = at(j, 0, 0)
        return remote(column(j, first), gath.at[s], s_c.at[j, dc], r_q.at[s, 0], at(0, 0, dc))

    def hb_send(j, dc, db):
        part = gath.at[at(j, 0, dc), pl.ds(0, half)]
        return remote(part, part, s_hb.at[j, dc, db], r_q.at[at(j, 0, dc), 0], at(0, db, 0))

    def hc_send(j, db, dc):
        part = gath.at[at(j, db, 0), pl.ds(half, half)]
        return remote(part, part, s_hc.at[j, db, dc], r_q.at[at(j, db, 0), 1], at(0, 0, dc))

    def res_send(s):
        return remote(res.at[s], ans.at[me], s_res.at[s], r_res.at[me], s)

    def rate_send(i):
        to = (me + i) % n
        return remote(rate_s, rate_v.at[me], s_rate.at[i], r_rate.at[me], to)

    def wait_block(s):
        remote(q_ref, gath.at[s], s_line.at[0], r_q.at[s, 0], me).wait_recv()

    def wait_half(s, k):
        part = gath.at[s, pl.ds(k * half, half)]
        remote(part, part, s_line.at[0], r_q.at[s, k], me).wait_recv()

    sibling = pltpu.make_async_remote_copy(
        src_ref=fresh_ref, dst_ref=fresh_v.at[1], send_sem=f_sem.at[0], recv_sem=f_sem.at[1],
        device_id=(1 - rep, me), device_id_type=MESH,
    )
    sibling_age = pltpu.make_async_remote_copy(
        src_ref=fages_ref, dst_ref=fage_v, send_sem=f_sem.at[2], recv_sem=f_sem.at[3],
        device_id=(1 - rep, me), device_id_type=MESH,
    )

    for dc in range(1, C):
        c_send(0, dc, True).start()
    for db in range(1, B):
        b_send(0, db, True).start()
    for j in range(1, A):
        line_send(j).start()

    @pl.loop(1, n)
    def _(i):
        rate_send(i).start()

    sibling_age.start()
    sibling.start()

    def spread(row):
        return jnp.transpose(jnp.broadcast_to(row.astype(jnp.float32), (ITEMS_BLOCK, ITEMS_BLOCK)))

    @pl.loop(0, main_rows)
    def _(k):
        age_v[pl.ds(pl.multiple_of(k * ITEMS_BLOCK, ITEMS_BLOCK), ITEMS_BLOCK), :] = spread(ages_ref[pl.ds(k, 1), :])

    rate_v[me] = rate_s[...]
    probes = jnp.transpose(probes_ref[...])

    def place_step(l, acc):
        return jnp.where(probes == l, place_ref[l], acc)

    slot_v[...] = lax.fori_loop(0, lists_n, place_step, jnp.zeros_like(probes))
    own_q.wait()
    own_items.wait()
    own_fresh.wait()

    other = (owner_ref[0] // n != rep).astype(jnp.int32)
    fresh_blocks = fresh_ref.shape[0] // ITEMS_BLOCK
    per_chunk = CHUNK // ITEMS_BLOCK

    def finish(dots, base, row0, s0, s1):
        age = age_v[pl.ds(base, CHUNK), :]
        for k, s in enumerate((s0, s1)):
            decay = jnp.exp2(age * rate_v[s, pl.ds(0, 1), :])
            scored = dots[:, k * rows:(k + 1) * rows] * decay
            best = jnp.max(scored.reshape(per_chunk, ITEMS_BLOCK, rows), axis=1)
            res[s, pl.ds(row0, per_chunk), :] = best

    def score(x, base, row0, s0, s1):
        dots = lax.dot_general(
            x, qp[...], (((1,), (1,)), ((), ())), preferred_element_type=jnp.float32
        )
        finish(dots, base, row0, s0, s1)

    pairs = B * C // 2
    front = max(1, C // 2) if pairs > 1 else pairs

    @pl.loop(0, A + 1)
    def _(j):
        @pl.when(j + 1 < A)
        def _():
            wait_block(at(j + 1, 0, 0))
            for dc in range(1, C):
                c_send(j + 1, dc).start()
            for db in range(1, B):
                b_send(j + 1, db).start()

        @pl.when(j < A)
        def _():
            for dc in range(1, C):
                wait_block(at(j, 0, dc))
                for db in range(1, B):
                    hb_send(j, dc, db).start()
            for db in range(1, B):
                wait_block(at(j, db, 0))
                for dc in range(1, C):
                    hc_send(j, db, dc).start()

        @pl.loop(0, pairs)
        def _(t):
            jj = jnp.where(t < front, j, j - 1)

            @pl.when((jj >= 0) & (jj < A))
            def _():
                s = []
                for k in range(2):
                    idx = 2 * t + k
                    db, dc = idx // C, idx % C
                    sk = at(jj, db, dc)
                    s.append(sk)

                    @pl.when((db > 0) & (dc > 0))
                    def _():
                        wait_half(sk, 0)
                        wait_half(sk, 1)

                    @pl.when(sk != me)
                    def _():
                        remote(rate_s, rate_v.at[sk], s_rate.at[0], r_rate.at[sk], me).wait_recv()

                    qp[k * rows:(k + 1) * rows, :] = gath[sk]
                s0, s1 = s

                @pl.loop(0, main_rows // per_chunk)
                def _(m):
                    base = pl.multiple_of(m * CHUNK, CHUNK)
                    score(item_v[pl.ds(base, CHUNK), :], base, pl.multiple_of(m * per_chunk, per_chunk), s0, s1)

                @pl.when((j == 0) & (t == 0))
                def _():
                    sibling.wait_recv()
                    sibling_age.wait_recv()
                    for k in range(fresh_blocks):
                        mine, theirs = fages_ref[k:k + 1, :], fage_v[k:k + 1, :]
                        row0 = (main_rows + k) * ITEMS_BLOCK
                        age_v[row0:row0 + ITEMS_BLOCK, :] = spread(jnp.where(other == 0, mine, theirs))

                score(fresh_v[other], main_rows * ITEMS_BLOCK, main_rows, s0, s1)
                for sk in s:
                    @pl.when(sk != me)
                    def _():
                        res_send(sk).start()

    ans[me] = res[me]

    def collect(i, acc):
        s = (me + i) % n

        @pl.when(s != me)
        def _():
            remote(res.at[s], ans.at[s], s_res.at[s], r_res.at[s], me).wait_recv()

        outs, fr = acc
        for sub in range(per_dev):
            part = ans[s, sub * blocks:(sub + 1) * blocks, :]
            outs = tuple(
                jnp.where(slot_v[p:p + 1, :] == s * per_dev + sub, part, o) for p, o in enumerate(outs)
            )
        fr = jnp.where(owner_ref[0] % n == s, ans[s, main_rows:main_rows + fresh_blocks, :], fr)
        return outs, fr

    zero = jnp.zeros((blocks, rows), jnp.float32)
    outs, fr = lax.fori_loop(
        0, n, collect,
        (tuple(zero for _ in range(probes_ref.shape[1])), jnp.zeros((fresh_blocks, rows), jnp.float32)),
    )
    out_ref[...] = jnp.transpose(jnp.concatenate(outs, axis=0))
    fout_ref[...] = jnp.transpose(fr)

    for j in range(A):
        for dc in range(1, C):
            c_send(j, dc, j == 0).wait_send()
        for db in range(1, B):
            b_send(j, db, j == 0).wait_send()
        if j > 0:
            line_send(j).wait_send()
        for dc in range(1, C):
            for db in range(1, B):
                hb_send(j, dc, db).wait_send()
                hc_send(j, db, dc).wait_send()

    @pl.loop(1, n)
    def _(i):
        rate_send(i).wait_send()
        res_send((me + i) % n).wait_send()

    sibling.wait_send()
    sibling_age.wait_send()


def shards(n, queries, rates, probes, list_place, items, ages, fresh_items, fresh_ages, owner):
    dims = grid_of(n)
    A, B, C = dims
    rows, width = queries.shape
    lists_n = list_place.shape[0]
    per_dev = lists_n // n
    item_n, fresh_n = items.shape[0], fresh_items.shape[0]
    main_rows, fresh_rows = item_n // ITEMS_BLOCK, fresh_n // ITEMS_BLOCK
    res_rows = main_rows + fresh_rows
    bf, f32, i32 = jnp.bfloat16, jnp.float32, jnp.int32
    scratch = [
        ((n, rows, width), bf), ((2 * rows, width), bf), ((item_n, width), bf),
        ((2, fresh_n, width), bf), ((fresh_rows, ITEMS_BLOCK), i32),
        ((item_n + fresh_n, ITEMS_BLOCK), f32), ((8, rows), f32), ((n, 8, rows), f32),
        ((probes.shape[1], rows), i32), ((n, res_rows, rows), f32), ((n, res_rows, rows), f32),
    ]
    used = sum(math.prod(shape) * jnp.dtype(kind).itemsize for shape, kind in scratch)
    dma = pltpu.SemaphoreType.DMA
    smem, vmem, hbm = (pl.BlockSpec(memory_space=m) for m in (pltpu.SMEM, pltpu.VMEM, pl.ANY))
    return pl.pallas_call(
        functools.partial(kernel, n, dims, lists_n, per_dev),
        out_shape=(
            jax.ShapeDtypeStruct((rows, probes.shape[1] * (main_rows // per_dev)), f32),
            jax.ShapeDtypeStruct((rows, fresh_rows), f32),
        ),
        in_specs=[smem, smem, vmem, vmem, vmem, vmem, hbm, hbm, hbm],
        out_specs=(vmem, vmem),
        scratch_shapes=[pltpu.VMEM(shape, kind) for shape, kind in scratch] + [
            dma((A,)), dma((A, B)), dma((A, C)), dma((A, C, B)), dma((A, B, C)),
            dma((n,)), dma((n,)), dma((n, 2)), dma((n,)), dma((n,)), dma((4,)), dma((3,)),
        ],
        compiler_params=pltpu.CompilerParams(
            collective_id=0, has_side_effects=True, vmem_limit_bytes=used + (10 << 20)
        ),
    )(
        owner, list_place, rates.reshape(1, rows), probes,
        ages.reshape(main_rows, ITEMS_BLOCK), fresh_ages.reshape(fresh_rows, ITEMS_BLOCK),
        queries, items, fresh_items,
    )


def solution(mesh):
    placed = (
        P(("rep", "lists"), None),
        P(("rep", "lists")),
        P(("rep", "lists"), None),
        P(),
        P("lists", None),
        P("lists"),
        P(("rep", "lists"), None),
        P(("rep", "lists")),
        P(),
    )
    return jax.shard_map(
        functools.partial(shards, mesh.shape["lists"]),
        mesh=mesh,
        in_specs=placed,
        out_specs=(P(("rep", "lists"), None), P(("rep", "lists"), None)),
        check_vma=False,
    )
```

```python
import functools
import math

import jax
import jax.numpy as jnp
from jax import lax
from jax.experimental import pallas as pl
from jax.experimental.pallas import tpu as pltpu
from jax.sharding import PartitionSpec as P

ITEMS_BLOCK = 128
CHUNK = 1024
LOG2E = math.log2(math.e)
MESH = pl.DeviceIdType.MESH


def grid_of(n):
    if n == 16:
        return 4, 2, 2
    if n == 128:
        return 4, 4, 8
    return n, 1, 1


def kernel(
    n, dims, lists_n, per_dev,
    owner_ref, place_ref, rates_ref, probes_hbm, ages_hbm, fages_hbm, q_ref, items_ref, fresh_ref,
    out_ref, fout_ref,
    gath, qp, item_v, fresh_v, fage_v, age_v, rate_s, rate_v, slot_v, res, ans, probes_ref, ages_ref, fages_ref,
    s_line, s_b, s_c, s_hb, s_hc, s_res, s_rate, r_q, r_res, r_rate, f_sem, l_sem,
):
    A, B, C = dims
    me = lax.axis_index("lists")
    rep = lax.axis_index("rep")
    a, b, c = me // (B * C), (me // C) % B, me % C
    rows = q_ref.shape[0]
    half = rows // 2
    list_rows = item_v.shape[0] // per_dev
    blocks = list_rows // ITEMS_BLOCK
    main_rows = per_dev * blocks

    def along(j):
        if A % 4:
            return (a + j) % A
        return (a // 4 * 4 + j // 4 * 4) % A + (a // 2 + j // 2) % 2 * 2 + (a + j) % 2

    def at(j, db, dc):
        return along(j) * (B * C) + ((b + db) % B) * C + (c + dc) % C

    def remote(src, dst, ss, rs, to):
        return pltpu.make_async_remote_copy(
            src_ref=src, dst_ref=dst, send_sem=ss, recv_sem=rs,
            device_id=(rep, to), device_id_type=MESH,
        )

    barrier = pltpu.get_barrier_semaphore()

    @pl.loop(1, n)
    def _(i):
        pl.semaphore_signal(barrier, inc=1, device_id=(rep, (me + i) % n), device_id_type=MESH)

    pl.semaphore_signal(barrier, inc=1, device_id=(1 - rep, me), device_id_type=MESH)

    own_q = pltpu.make_async_copy(q_ref, gath.at[me], l_sem.at[0])
    own_items = pltpu.make_async_copy(items_ref, item_v, l_sem.at[1])
    own_fresh = pltpu.make_async_copy(fresh_ref, fresh_v.at[0], l_sem.at[2])
    small = [
        pltpu.make_async_copy(src, dst, l_sem.at[3 + i])
        for i, (src, dst) in enumerate(((ages_hbm, ages_ref), (fages_hbm, fages_ref), (probes_hbm, probes_ref)))
    ]
    for copy in small:
        copy.start()
    own_q.start()
    own_items.start()
    own_fresh.start()
    rate_s[...] = jnp.broadcast_to(rates_ref[...].astype(jnp.float32) * (-LOG2E), rate_s.shape)
    pl.semaphore_wait(barrier, n)

    def line_send(j):
        return remote(q_ref, gath.at[me], s_line.at[j], r_q.at[me, 0], at(j, 0, 0))

    def column(j, first):
        s = at(j, 0, 0)
        return q_ref if first else gath.at[s]

    def b_send(j, db, first=False):
        s = at(j, 0, 0)
        return remote(column(j, first), gath.at[s], s_b.at[j, db], r_q.at[s, 0], at(0, db, 0))

    def c_send(j, dc, first=False):
        s = at(j, 0, 0)
        return remote(column(j, first), gath.at[s], s_c.at[j, dc], r_q.at[s, 0], at(0, 0, dc))

    def hb_send(j, dc, db):
        part = gath.at[at(j, 0, dc), pl.ds(0, half)]
        return remote(part, part, s_hb.at[j, dc, db], r_q.at[at(j, 0, dc), 0], at(0, db, 0))

    def hc_send(j, db, dc):
        part = gath.at[at(j, db, 0), pl.ds(half, half)]
        return remote(part, part, s_hc.at[j, db, dc], r_q.at[at(j, db, 0), 1], at(0, 0, dc))

    def res_send(s):
        return remote(res.at[s], ans.at[me], s_res.at[s], r_res.at[me], s)

    def rate_send(i):
        to = (me + i) % n
        return remote(rate_s, rate_v.at[me], s_rate.at[i], r_rate.at[me], to)

    def wait_block(s):
        remote(q_ref, gath.at[s], s_line.at[0], r_q.at[s, 0], me).wait_recv()

    def wait_half(s, k):
        part = gath.at[s, pl.ds(k * half, half)]
        remote(part, part, s_line.at[0], r_q.at[s, k], me).wait_recv()

    sibling = pltpu.make_async_remote_copy(
        src_ref=fresh_ref, dst_ref=fresh_v.at[1], send_sem=f_sem.at[0], recv_sem=f_sem.at[1],
        device_id=(1 - rep, me), device_id_type=MESH,
    )
    sibling_age = pltpu.make_async_remote_copy(
        src_ref=fages_hbm, dst_ref=fage_v, send_sem=f_sem.at[2], recv_sem=f_sem.at[3],
        device_id=(1 - rep, me), device_id_type=MESH,
    )

    for dc in range(1, C):
        c_send(0, dc, True).start()
    for db in range(1, B):
        b_send(0, db, True).start()
    for j in range(1, A):
        line_send(j).start()

    @pl.loop(1, n)
    def _(i):
        rate_send(i).start()

    sibling_age.start()
    sibling.start()

    for copy in small:
        copy.wait()

    def spread(row):
        return jnp.transpose(jnp.broadcast_to(row.astype(jnp.float32), (ITEMS_BLOCK, ITEMS_BLOCK)))

    @pl.loop(0, main_rows)
    def _(k):
        age_v[pl.ds(pl.multiple_of(k * ITEMS_BLOCK, ITEMS_BLOCK), ITEMS_BLOCK), :] = spread(ages_ref[pl.ds(k, 1), :])

    rate_v[me] = rate_s[...]
    probes = probes_ref[...]

    def place_step(l, acc):
        return jnp.where(probes == l, place_ref[l], acc)

    slot_v[...] = lax.fori_loop(0, lists_n, place_step, jnp.zeros_like(probes))
    own_q.wait()
    own_items.wait()
    own_fresh.wait()

    other = (owner_ref[0] // n != rep).astype(jnp.int32)
    fresh_blocks = fresh_ref.shape[0] // ITEMS_BLOCK
    per_chunk = CHUNK // ITEMS_BLOCK

    def finish(dots, base, row0, s0, s1):
        age = age_v[pl.ds(base, CHUNK), :]
        for k, s in enumerate((s0, s1)):
            decay = jnp.exp2(age * rate_v[s, pl.ds(0, 1), :])
            scored = dots[:, k * rows:(k + 1) * rows] * decay
            best = jnp.max(scored.reshape(per_chunk, ITEMS_BLOCK, rows), axis=1)
            res[s, pl.ds(row0, per_chunk), :] = best

    def score(x, base, row0, s0, s1):
        dots = lax.dot_general(
            x, qp[...], (((1,), (1,)), ((), ())), preferred_element_type=jnp.float32
        )
        finish(dots, base, row0, s0, s1)

    pairs = B * C // 2
    front = max(1, C // 2) if pairs > 1 else pairs

    @pl.loop(0, A + 1)
    def _(j):
        @pl.when(j < A)
        def _():
            for dc in range(1, C):
                wait_block(at(j, 0, dc))
                for db in range(1, B):
                    hb_send(j, dc, db).start()
            for db in range(1, B):
                wait_block(at(j, db, 0))
                for dc in range(1, C):
                    hc_send(j, db, dc).start()

        @pl.when(j + 1 < A)
        def _():
            wait_block(at(j + 1, 0, 0))
            for dc in range(1, C):
                c_send(j + 1, dc).start()
            for db in range(1, B):
                b_send(j + 1, db).start()

        @pl.loop(0, pairs)
        def _(t):
            jj = jnp.where(t < front, j, j - 1)

            @pl.when((jj >= 0) & (jj < A))
            def _():
                s = []
                for k in range(2):
                    idx = 2 * t + k
                    db, dc = idx // C, idx % C
                    sk = at(jj, db, dc)
                    s.append(sk)

                    @pl.when((db > 0) & (dc > 0))
                    def _():
                        wait_half(sk, 0)
                        wait_half(sk, 1)

                    @pl.when(sk != me)
                    def _():
                        remote(rate_s, rate_v.at[sk], s_rate.at[0], r_rate.at[sk], me).wait_recv()

                    qp[k * rows:(k + 1) * rows, :] = gath[sk]
                s0, s1 = s

                @pl.loop(0, main_rows // per_chunk)
                def _(m):
                    base = pl.multiple_of(m * CHUNK, CHUNK)
                    score(item_v[pl.ds(base, CHUNK), :], base, pl.multiple_of(m * per_chunk, per_chunk), s0, s1)

                @pl.when((j == 0) & (t == 0))
                def _():
                    sibling.wait_recv()
                    sibling_age.wait_recv()
                    for k in range(fresh_blocks):
                        mine, theirs = fages_ref[k:k + 1, :], fage_v[k:k + 1, :]
                        row0 = (main_rows + k) * ITEMS_BLOCK
                        age_v[row0:row0 + ITEMS_BLOCK, :] = spread(jnp.where(other == 0, mine, theirs))

                score(fresh_v[other], main_rows * ITEMS_BLOCK, main_rows, s0, s1)
                for sk in s:
                    @pl.when(sk != me)
                    def _():
                        res_send(sk).start()

    ans[me] = res[me]

    def collect(i, acc):
        s = (me + i) % n

        @pl.when(s != me)
        def _():
            remote(res.at[s], ans.at[s], s_res.at[s], r_res.at[s], me).wait_recv()

        outs, fr = acc
        for sub in range(per_dev):
            part = ans[s, sub * blocks:(sub + 1) * blocks, :]
            outs = tuple(
                jnp.where(slot_v[p:p + 1, :] == s * per_dev + sub, part, o) for p, o in enumerate(outs)
            )
        fr = jnp.where(owner_ref[0] % n == s, ans[s, main_rows:main_rows + fresh_blocks, :], fr)
        return outs, fr

    zero = jnp.zeros((blocks, rows), jnp.float32)
    outs, fr = lax.fori_loop(
        0, n, collect,
        (tuple(zero for _ in range(probes_ref.shape[0])), jnp.zeros((fresh_blocks, rows), jnp.float32)),
    )
    out_ref[...] = jnp.transpose(jnp.concatenate(outs, axis=0))
    fout_ref[...] = fr

    for j in range(A):
        for dc in range(1, C):
            c_send(j, dc, j == 0).wait_send()
        for db in range(1, B):
            b_send(j, db, j == 0).wait_send()
        if j > 0:
            line_send(j).wait_send()
        for dc in range(1, C):
            for db in range(1, B):
                hb_send(j, dc, db).wait_send()
                hc_send(j, db, dc).wait_send()

    @pl.loop(1, n)
    def _(i):
        rate_send(i).wait_send()
        res_send((me + i) % n).wait_send()

    sibling.wait_send()
    sibling_age.wait_send()


def shards(n, queries, rates, probes, list_place, items, ages, fresh_items, fresh_ages, owner):
    dims = grid_of(n)
    A, B, C = dims
    rows, width = queries.shape
    lists_n = list_place.shape[0]
    per_dev = lists_n // n
    item_n, fresh_n = items.shape[0], fresh_items.shape[0]
    main_rows, fresh_rows = item_n // ITEMS_BLOCK, fresh_n // ITEMS_BLOCK
    res_rows = main_rows + fresh_rows
    bf, f32, i32 = jnp.bfloat16, jnp.float32, jnp.int32
    scratch = [
        ((n, rows, width), bf), ((2 * rows, width), bf), ((item_n, width), bf),
        ((2, fresh_n, width), bf), ((fresh_rows, ITEMS_BLOCK), i32),
        ((item_n + fresh_n, ITEMS_BLOCK), f32), ((8, rows), f32), ((n, 8, rows), f32),
        ((probes.shape[1], rows), i32), ((n, res_rows, rows), f32), ((n, res_rows, rows), f32),
        ((probes.shape[1], rows), i32), ((main_rows, ITEMS_BLOCK), i32), ((fresh_rows, ITEMS_BLOCK), i32),
    ]
    dma = pltpu.SemaphoreType.DMA
    smem, vmem, hbm = (pl.BlockSpec(memory_space=m) for m in (pltpu.SMEM, pltpu.VMEM, pl.ANY))
    best, fresh = pl.pallas_call(
        functools.partial(kernel, n, dims, lists_n, per_dev),
        out_shape=(
            jax.ShapeDtypeStruct((rows, probes.shape[1] * (main_rows // per_dev)), f32),
            jax.ShapeDtypeStruct((fresh_rows, rows), f32),
        ),
        in_specs=[smem, smem, vmem] + [hbm] * 6,
        out_specs=(vmem, vmem),
        scratch_shapes=[pltpu.VMEM(shape, kind) for shape, kind in scratch] + [
            dma((A,)), dma((A, B)), dma((A, C)), dma((A, C, B)), dma((A, B, C)),
            dma((n,)), dma((n,)), dma((n, 2)), dma((n,)), dma((n,)), dma((4,)), dma((6,)),
        ],
        compiler_params=pltpu.CompilerParams(
            collective_id=0, has_side_effects=True, vmem_limit_bytes=63 << 20
        ),
    )(
        owner, list_place, rates.reshape(1, rows), probes.T,
        ages.reshape(main_rows, ITEMS_BLOCK), fresh_ages.reshape(fresh_rows, ITEMS_BLOCK),
        queries, items, fresh_items,
    )
    return best, fresh.T


def solution(mesh):
    placed = (
        P(("rep", "lists"), None),
        P(("rep", "lists")),
        P(("rep", "lists"), None),
        P(),
        P("lists", None),
        P("lists"),
        P(("rep", "lists"), None),
        P(("rep", "lists")),
        P(),
    )
    return jax.shard_map(
        functools.partial(shards, mesh.shape["lists"]),
        mesh=mesh,
        in_specs=placed,
        out_specs=(P(("rep", "lists"), None), P(("rep", "lists"), None)),
        check_vma=False,
    )
```
